256 devices in a mesh: leaf: 16 (over y, x), far: 16 (over z, core).
Axes of the slice: x: 4, y: 4, z: 8, core: 2. Of those that a mesh axis runs over, the one named last changes fastest.
Arguments:
- right_sides: bfloat16 [16, 64, 131072], P('far', None, 'leaf'), may hold values from -6 to 6
- point_coords: bfloat16 [16, 3, 131072], P('far', None, 'leaf'), may hold values from 0 to 1
- near_offsets: int32 [16, 1024, 24], P('far', 'leaf'), may hold values from -16 to 16
- leaf_basis: bfloat16 [16, 64, 131072], P('far', None, 'leaf'), may hold values from -0.5 to 0.5
- local_transfer: bfloat16 [16, 2016, 64, 64], P('far', 'leaf'), may hold values from -0.75 to 0.75
- top_transfer: bfloat16 [16, 30, 64, 64], P('far'), may hold values from -0.75 to 0.75
- coupling_pattern: int32 [16, 1008, 4], P('far', 'leaf'), may hold values from 0 to 15, all different within a row; in each aligned block of 63 rows (0 to 62, 63 to 125, ..., all dimensions but the last counted through in order) at most 32 rows name the same one
- coupling_blocks: bfloat16 [16, 1008, 4, 64, 64], P('far', 'leaf'), may hold values from -0.375 to 0.375
- root_pattern: int32 [16, 16], P('far'), may hold values 0 or 1
- root_blocks: bfloat16 [16, 16, 64, 64], P('far'), may hold values from -0.25 to 0.25
Outputs:
- potential: bfloat16 [16, 64, 131072], P('far', None, 'leaf')
The draws below stay inside these ranges and needn't reach their ends.
Inputs may be any that keep to these rules, and one draw needn't show every extreme that they name: `coupling_pattern`: each row names 4 different partitions; among the rows of one subtree no partition is named more than 32 times, a bound that some block reaches.
All inputs are finite; a program needn't handle non-finite values. No bound on the sum of `root_pattern` on one device may be relied on, other than what follows from the above.
Results may differ from the reference program's by a relative error of at most 0.028.
Values may be sent and summed in bfloat16 or wider, within the bound.
A program may use at most 128 MiB of HBM per device.

```python
import math
import jax
import jax.numpy as jnp
import numpy as np
from jax import lax

R = 64
NRHS = 64
P_SIZE = 128
LEAF_DEV = 64
NEAR = 24
HALO = 16
KC = 4
NODES = 63
LEAVES = 1024
NPTS = 131072
TOPCH = 30
CAP = 32
TOP_LEVELS = 4
LOCAL_LEVELS = 6
N_LEAF = 16
N_FAR = 16


def place_ends(result, rng, smallest, top_value):
    extent = result.shape
    spot = [jax.random.randint(jax.random.fold_in(rng, axis), (), 0, extent[axis]) for axis in range(len(extent))]
    result = result.at[tuple(spot)].set(smallest)
    longest = extent.index(max(extent))
    spot[longest] = (spot[longest] + 1) % extent[longest]
    return result.at[tuple(spot)].set(top_value)


def level_of(key, shape, cuts, least, high):
    factor_of = 1.0
    for dim, blocks in cuts:
        heights = jax.random.uniform(jax.random.fold_in(jax.random.fold_in(key, 6), dim), (blocks,), jnp.float32, least / len(cuts), high / len(cuts))
        factor_of = factor_of * jnp.repeat(jnp.exp(heights), shape[dim] // blocks).reshape((-1,) + (1,) * (len(shape) - 1 - dim))
    return factor_of


def shared_out(stream_key, own, number, rows, number_of, top, bound, lean):
    sequence = jax.random.permutation(stream_key, number_of)
    heavy_load, ordinary = portions_of(number_of, rows * top, bound, lean, True), portions_of(number_of, rows * top, bound, lean, False)
    places = jnp.arange(number_of)

    def named(tallies, rotation):
        used = int((tallies > 0).sum())
        fixed = max(1, used // 4)
        shifted = fixed + (places - fixed + rotation * (used - fixed)) % max(1, number_of - fixed)
        return jnp.zeros((number_of,), jnp.int32).at[sequence[jnp.where(places < fixed, places, shifted)]].set(jnp.asarray(tallies, jnp.int32))

    tallies = jnp.where(number % 4 == 0, named(heavy_load, number // 4), named(ordinary, number - number // 4 - 1))
    mixed = jax.random.permutation(jax.random.fold_in(own, 3), number_of)
    giver, receiver = mixed[0:number_of // 2 * 2:2], mixed[1:number_of // 2 * 2:2]
    room = jnp.minimum(tallies[giver] - 1, bound - tallies[receiver]) // 2
    room = jnp.where((giver == sequence[0]) | (receiver == sequence[0]) | (tallies[receiver] == 0), 0, jnp.maximum(room, 0))
    shifted = jax.random.randint(jax.random.fold_in(own, 4), (number_of // 2,), 0, 1 << 20) % (room + 1)
    tallies = tallies.at[giver].add(-shifted).at[receiver].add(shifted)
    labels = jnp.searchsorted(jnp.cumsum(tallies), jnp.arange(rows * top), side="right").astype(jnp.int32)
    table = labels.reshape(top, rows).T
    table = table[jax.random.permutation(jax.random.fold_in(own, 1), rows)]
    rotation = jax.random.randint(jax.random.fold_in(own, 2), (rows, 1), 0, top)
    return jnp.take_along_axis(table, (jnp.arange(top)[None, :] + rotation) % top, axis=1)


def portions_of(count, total, limit, slope, full):
    portions = [(1 << 20) // math.isqrt(rank ** slope) + 1 for rank in range(1, count + 1)]
    largest = limit if full else min(limit, max(-(-total // count), total * portions[0] // sum(portions)))
    least = 1 if total - largest >= count - 1 else 0
    counts, spare = [largest] + [least] * (count - 1), total - largest - least * (count - 1)
    while spare > 0:
        candidates = [i for i in range(1, count) if counts[i] < largest] or [i for i in range(1, count) if counts[i] < limit]
        mass, left = sum([portions[i] for i in candidates]), spare
        for i in candidates:
            extra = min(limit - counts[i], max(1, left * portions[i] // mass), spare)
            counts[i] = counts[i] + extra
            spare = spare - extra
    return np.array(counts)


def centred(own_key, shape, width, limit, cuts=(), kind=jnp.bfloat16):
    result = jax.random.normal(own_key, shape, jnp.float32) * width
    if len(cuts) > 0:
        result = level_of(own_key, shape, cuts, -0.22, 0.18) * result
    return jnp.clip(result, min=-limit, max=limit).astype(kind)


def setup_inputs(seed: int = 0) -> dict:
    splits = jax.random.split(jax.random.key(seed), 11)
    right_sides = centred(splits[0], (N_FAR, NRHS, NPTS), 1.0, 6.0, ((0, 16), (2, 16)))
    point_coords = jnp.clip(1.0 * jax.random.uniform(splits[1], (N_FAR, 3, NPTS), jnp.float32) ** level_of(splits[1], (N_FAR, 3, NPTS), ((0, 16), (2, 16)), -0.2, 0.2), 0.0, 1.0).astype(jnp.bfloat16)
    near_offsets = place_ends(jax.random.randint(splits[2], (N_FAR, LEAVES, NEAR), 0 - HALO, HALO + 1), jax.random.fold_in(splits[2], 1), 0 - HALO, HALO).astype(jnp.int32)
    leaf_basis = centred(splits[3], (N_FAR, R, NPTS), P_SIZE ** -0.5, 0.5, ((0, 16), (2, 16)))
    local_transfer = centred(splits[4], (N_FAR, N_LEAF * 2 * NODES, R, R), R ** -0.5, 0.75, ((0, 16), (1, 16)))
    top_transfer = centred(splits[5], (N_FAR, TOPCH, R, R), R ** -0.5, 0.75, ((0, 16),))
    coupling_pattern_keys = jax.random.split(jax.random.fold_in(splits[6], 1), N_FAR * (N_LEAF * NODES) // NODES)
    coupling_pattern_turns = jax.random.permutation(jax.random.fold_in(splits[6], 3), N_FAR * (N_LEAF * NODES) // NODES)
    coupling_pattern = jax.vmap(lambda own, number: shared_out(jax.random.fold_in(splits[6], 2), own, number, NODES, N_FAR, KC, CAP, 2))(coupling_pattern_keys, coupling_pattern_turns).reshape((N_FAR, N_LEAF * NODES, KC))
    coupling_blocks = centred(splits[7], (N_FAR, N_LEAF * NODES, KC, R, R), (R * KC) ** -0.5, 0.375, ((0, 16), (1, 16)))
    root_pattern = place_ends((jax.random.randint(splits[8], (N_FAR, N_FAR), 0, 2) < 1).astype(jnp.int32), jax.random.fold_in(splits[8], 1), 0, 1)
    root_blocks = centred(splits[9], (N_FAR, N_FAR, R, R), (R * N_FAR // 2) ** -0.5, 0.25, ((0, 16),))
    return dict(right_sides=right_sides, point_coords=point_coords, near_offsets=near_offsets, leaf_basis=leaf_basis, local_transfer=local_transfer, top_transfer=top_transfer, coupling_pattern=coupling_pattern, coupling_blocks=coupling_blocks, root_pattern=root_pattern, root_blocks=root_blocks)


HALF_ROOT = 0.7071067811865476
SOFTEN = 0.0004
HIGHEST_PREC = lax.Precision.HIGHEST

def to_half(values):
    return lax.optimization_barrier(values.astype(jnp.bfloat16)).astype(jnp.float32)

def kernel_block(targets, sources, factor):
    squared = jnp.zeros(targets.shape[1:] + (sources.shape[2],), jnp.float32)
    for component in range(3):
        spacing = targets[component][:, :, None] - sources[component][:, None, :]
        squared = squared + spacing * spacing
    return (factor / jnp.sqrt(squared + SOFTEN)).astype(jnp.bfloat16)

def level_starts(first, levels):
    starts = []
    offset = 0
    for level_at in range(levels):
        starts.append(offset)
        offset = offset + (first >> level_at)
    return starts

def near_field(point_values, points, offsets):
    leaf_count = point_values.shape[1]
    factor = 1.0 / math.sqrt(offsets.shape[1] * point_values.shape[2])
    indices = jnp.arange(leaf_count, dtype=jnp.int32)

    def advance(running, column):
        source = indices + column
        inside = (source >= 0) & (source < leaf_count)
        clipped = jnp.clip(source, 0, leaf_count - 1).astype(jnp.int32)
        picked = jnp.where(inside[None, :, None], point_values[:, clipped], jnp.zeros((), point_values.dtype))
        kernel = kernel_block(points, points[:, clipped], factor)
        addend = jnp.einsum('sib,iab->sia', picked.astype(jnp.float32), kernel.astype(jnp.float32))
        return (running + addend, None)
    running, unused = lax.scan(advance, jnp.zeros(point_values.shape, jnp.float32), offsets.T)
    return running

def local_upsweep(point_values, cluster_basis_rows, transfer):
    present_level_value = jnp.einsum('ypb,kpb->pyk', point_values.astype(jnp.float32), cluster_basis_rows.astype(jnp.float32))
    present_level_value = present_level_value.reshape(N_LEAF, LEAF_DEV, NRHS, R)
    starts = level_starts(LEAF_DEV, LOCAL_LEVELS)
    levels = []
    for level_at in range(LOCAL_LEVELS):
        width_now = LEAF_DEV >> level_at
        matrices = transfer[:, starts[level_at]:starts[level_at] + width_now].astype(jnp.float32)
        mapped = jnp.einsum('njsr,njrt->njst', to_half(present_level_value), matrices, precision=HIGHEST_PREC)
        present_level_value = (mapped[:, 0::2] + mapped[:, 1::2]) * HALF_ROOT
        levels.append(present_level_value)
    return jnp.concatenate(levels, axis=1)

def reference(right_sides, point_coords, near_offsets, leaf_basis, local_transfer, top_transfer, coupling_pattern, coupling_blocks, root_pattern, root_blocks):
    values_all = right_sides.reshape(N_FAR, NRHS, LEAVES, P_SIZE)
    bases_all = leaf_basis.reshape(N_FAR, R, LEAVES, P_SIZE)
    transfer_all = local_transfer.reshape(N_FAR, N_LEAF, 2 * NODES, R, R)
    node_coef = lax.map(lambda entries: local_upsweep(entries[0], entries[1], entries[2]), (values_all, bases_all, transfer_all))
    top_starts = level_starts(N_LEAF, TOP_LEVELS)
    present_level_value = node_coef[:, :, NODES - 1]
    for level_at in range(TOP_LEVELS):
        width_now = N_LEAF >> level_at
        matrices = top_transfer[:, top_starts[level_at]:top_starts[level_at] + width_now].astype(jnp.float32)
        mapped = jnp.einsum('fgsr,fgrt->fgst', to_half(present_level_value), matrices, precision=HIGHEST_PREC)
        present_level_value = (mapped[:, 0::2] + mapped[:, 1::2]) * HALF_ROOT
    roots = present_level_value[:, 0]
    root_local = jnp.einsum('fp,psr,fprt->fst', root_pattern.astype(jnp.float32), to_half(roots), root_blocks.astype(jnp.float32), precision=HIGHEST_PREC)
    present_level_value = root_local[:, None]
    for level_at in reversed(range(TOP_LEVELS)):
        width_now = N_LEAF >> level_at
        matrices = top_transfer[:, top_starts[level_at]:top_starts[level_at] + width_now].astype(jnp.float32)
        present_level_value = jnp.einsum('fgsr,fgtr->fgst', to_half(jnp.repeat(present_level_value, 2, axis=1)), matrices, precision=HIGHEST_PREC)
    subtree_local = present_level_value
    rounded = node_coef.astype(jnp.bfloat16)
    subtree_index = jnp.arange(N_LEAF, dtype=jnp.int32)[:, None, None]
    node_index = jnp.arange(NODES, dtype=jnp.int32)[None, :, None]

    def couple_partition(entries):
        pattern = entries[0].reshape(N_LEAF, NODES, KC).astype(jnp.int32)
        sources = rounded[pattern, subtree_index, node_index]
        matrices = entries[1].reshape(N_LEAF, NODES, KC, R, R)
        return jnp.einsum('njksr,njkrt->njst', sources.astype(jnp.float32), matrices.astype(jnp.float32))
    gains = lax.map(couple_partition, (coupling_pattern, coupling_blocks))
    local_starts = level_starts(LEAF_DEV, LOCAL_LEVELS)
    node_starts = level_starts(LEAF_DEV // 2, LOCAL_LEVELS)

    def finish_partition(entries):
        point_values, points, offsets, cluster_basis_rows, transfer, descent, gain_rows = entries
        present_level_value = descent[:, None]
        for level_at in range(LOCAL_LEVELS, 0, -1):
            width_now = LEAF_DEV >> level_at
            first_node = node_starts[level_at - 1]
            present_level_value = present_level_value + gain_rows[:, first_node:first_node + width_now]
            first_child = local_starts[level_at - 1]
            matrices = transfer[:, first_child:first_child + 2 * width_now].astype(jnp.float32)
            present_level_value = jnp.einsum('njsr,njtr->njst', to_half(jnp.repeat(present_level_value, 2, axis=1)), matrices, precision=HIGHEST_PREC)
        leaf_local_coef = present_level_value.reshape(LEAVES, NRHS, R).astype(jnp.bfloat16)
        farfield_sum = jnp.einsum('bhv,vbu->hbu', leaf_local_coef.astype(jnp.float32), cluster_basis_rows.astype(jnp.float32))
        near_sum = near_field(point_values, points, offsets)
        return (near_sum + farfield_sum).astype(jnp.bfloat16).reshape(NRHS, NPTS)
    points_all = point_coords.reshape(N_FAR, 3, LEAVES, P_SIZE).astype(jnp.float32)
    return lax.map(finish_partition, (values_all, points_all, near_offsets, bases_all, transfer_all, subtree_local, gains))
```

```python
import functools
import math

import jax
import jax.numpy as jnp
from jax import lax
from jax.experimental import pallas as pl
from jax.experimental.pallas import tpu as pltpu
from jax.sharding import PartitionSpec as P

BF = jnp.bfloat16
F32 = jnp.float32
MESH = pl.DeviceIdType.MESH
HALO = 16
HALF_ROOT = 0.7071067811865476
SOFTEN = 0.0004
LEAVES = 64
WINDOW = LEAVES + 2 * HALO
P_SIZE = 128
RANK = 64
NEAR = 24
KC = 4
N_LEAF = 16
N_FAR = 16
PAIRS = LEAVES // 2
NODES = LEAVES - 1
BLOCKS = 32
PIECE = BLOCKS // 2
RING = N_FAR // 2
STEPS = 7
FEATS = 16
CHILD_START = (0, 64, 96, 112, 120, 124)
ROW_START = (None, 0, 32, 48, 56, 60, 62)
TOP_START = (0, 16, 24, 28)


def lanes(index, count=1):
    return pl.ds(pl.multiple_of(index * P_SIZE, P_SIZE), count * P_SIZE)


def split3(value):
    high = value.astype(BF).astype(F32)
    rest = value - high
    middle = rest.astype(BF).astype(F32)
    return high, middle, rest - middle


def stacked_rows(rows, width):
    at = lax.broadcasted_iota(jnp.int32, (FEATS, width), 0)
    out = jnp.zeros((FEATS, width), F32)
    for r, row in enumerate(rows):
        out = jnp.where(at == r, row, out)
    return out.astype(BF)


def kernel(
    offsets,
    pattern,
    root_pattern,
    coords,
    tops,
    x_hbm,
    basis_hbm,
    transfer_hbm,
    coupling_hbm,
    root_blocks_hbm,
    out_hbm,
    window,
    target_feats,
    target_turned,
    basis,
    transfer,
    coupling,
    root_blocks,
    h0,
    gathered,
    roots,
    tops_in,
    descent,
    gains,
    expansion,
    near_sum,
    out_vmem,
    load_sem,
    x_sem,
    halo_send,
    halo_recv,
    ring_send,
    ring_recv,
    sib_send,
    sib_recv,
    root_send,
    root_recv,
    top_send,
    top_recv,
):
    leaf = lax.axis_index("leaf")
    far = lax.axis_index("far")
    z = far // 2
    core = lax.rem(far, 2)
    sibling = z * 2 + (1 - core)

    def column(step):
        return lax.rem(z + RING + step, RING) * 2 + core

    def leaf_peer(k):
        return lax.rem(leaf + k + N_LEAF, N_LEAF)

    def far_peer(k):
        return lax.rem(far + k + N_FAR, N_FAR)

    barrier = pltpu.get_barrier_semaphore()
    for k in range(1, N_LEAF):
        pl.semaphore_signal(
            barrier, inc=1, device_id=(leaf_peer(k), far), device_id_type=MESH
        )
    for k in range(1, N_FAR):
        pl.semaphore_signal(
            barrier, inc=1, device_id=(leaf, far_peer(k)), device_id_type=MESH
        )

    def load_x(i):
        return pltpu.make_async_copy(
            x_hbm.at[:, lanes(i)], window.at[HALO + i, pl.ds(0, RANK)], x_sem.at[i]
        )

    def start_x(i, carry):
        load_x(i).start()
        return carry

    def wait_x(i, carry):
        load_x(i).wait()
        return carry

    lax.fori_loop(0, LEAVES, start_x, 0)
    load_basis = pltpu.make_async_copy(basis_hbm, basis, load_sem.at[1])
    load_basis.start()
    load_transfer = pltpu.make_async_copy(transfer_hbm, transfer, load_sem.at[2])
    load_transfer.start()
    load_coupling = pltpu.make_async_copy(coupling_hbm, coupling, load_sem.at[3])
    load_root_blocks = pltpu.make_async_copy(root_blocks_hbm, root_blocks, load_sem.at[4])
    load_coupling.start()
    load_root_blocks.start()

    chunk = 1024

    def make_feats(q, carry):
        at = pl.ds(pl.multiple_of(q * chunk, chunk), chunk)
        c = coords[:, at].astype(F32)
        rows = [c[r : r + 1] for r in range(3)]
        square = rows[0] * rows[0] + rows[1] * rows[1] + rows[2] * rows[2]
        one = jnp.ones_like(square)
        feats = stacked_rows([*rows, one, one, one, *split3(square)], chunk)
        for t in range(chunk // P_SIZE):
            window[HALO + q * (chunk // P_SIZE) + t, RANK : RANK + FEATS] = feats[
                :, t * P_SIZE : (t + 1) * P_SIZE
            ]
        target_feats[:, at] = stacked_rows(
            [*(-2.0 * row for row in rows), *split3(square + SOFTEN), one, one, one], chunk
        )
        return carry

    lax.fori_loop(0, LEAVES * P_SIZE // chunk, make_feats, 0)
    lax.fori_loop(0, LEAVES, wait_x, 0)
    pl.semaphore_wait(barrier, N_LEAF - 1 + N_FAR - 1)

    halo = []
    for way, (src, dst) in enumerate(((LEAVES, 0), (HALO, LEAVES + HALO))):
        copy = pltpu.make_async_remote_copy(
            src_ref=window.at[pl.ds(src, HALO)],
            dst_ref=window.at[pl.ds(dst, HALO)],
            send_sem=halo_send.at[way],
            recv_sem=halo_recv.at[way],
            device_id=(leaf_peer(1 if way == 0 else -1), far),
            device_id_type=MESH,
        )
        copy.start()
        halo.append(copy)

    load_basis.wait()

    def leaf_pair(q, carry):
        parts = []
        for t in range(2):
            x = window[HALO + 2 * q + t, 0:RANK]
            b = basis[:, lanes(2 * q + t)]
            parts.append(
                lax.dot_general(
                    x, b, (((1,), (1,)), ((), ())), preferred_element_type=F32
                )
            )
        h0[q] = jnp.concatenate(parts, axis=1).astype(BF)
        return carry

    lax.fori_loop(0, PAIRS, leaf_pair, 0, unroll=8)
    load_transfer.wait()

    def piece_of(way, step):
        return 1 - lax.rem(step, 2) if way == 1 else lax.rem(step, 2)

    def ring_copy(way, step):
        piece = piece_of(way, step)
        behind = step // 2
        block = gathered.at[
            column(-behind if way == 0 else behind), pl.ds(piece * PIECE, PIECE)
        ]
        return pltpu.make_async_remote_copy(
            src_ref=block,
            dst_ref=block,
            send_sem=ring_send.at[way, step],
            recv_sem=ring_recv.at[way, step],
            device_id=(leaf, column(1 if way == 0 else -1)),
            device_id_type=MESH,
        )

    def sib_copy(way, step):
        piece = piece_of(way, step)
        behind = step // 2 + 1
        part = far if way == 2 else column(-behind if way == 0 else behind)
        block = gathered.at[part, pl.ds(piece * PIECE, PIECE)]
        return pltpu.make_async_remote_copy(
            src_ref=block,
            dst_ref=block,
            send_sem=sib_send.at[way, step],
            recv_sem=sib_recv.at[way, step],
            device_id=(leaf, sibling),
            device_id_type=MESH,
        )

    def up_node(source, first_child, j):
        e = transfer[pl.ds(first_child + 2 * j, 2)].reshape(2 * RANK, RANK)
        return jnp.dot(source[j], e, preferred_element_type=F32) * HALF_ROOT

    def up_level(level, source, first_block):
        first_child = CHILD_START[level - 1]

        def pair(q, carry):
            both = [up_node(source, first_child, 2 * q + t) for t in range(2)]
            gathered[far, first_block + q] = jnp.concatenate(both, axis=1).astype(BF)
            return carry

        count = LEAVES >> (level + 1)
        lax.fori_loop(0, count, pair, 0, unroll=min(count, 8))

    mine = gathered.at[far]
    up_level(1, h0, 0)
    ring_copy(0, 0).start()
    ring_copy(1, 1).start()
    sib_copy(2, 0).start()
    for level in range(2, 6):
        up_level(
            level,
            mine.at[pl.ds(ROW_START[level - 1] // 2, LEAVES >> level)],
            ROW_START[level] // 2,
        )
    root = up_node(mine.at[pl.ds(ROW_START[5] // 2, 1)], CHILD_START[5], 0).astype(BF)
    root = jnp.concatenate([root, jnp.zeros_like(root)], axis=1)
    gathered[far, BLOCKS - 1] = root
    roots[leaf] = root
    ring_copy(0, 1).start()
    ring_copy(1, 0).start()
    root_copies = []
    for k in range(1, N_LEAF):
        copy = pltpu.make_async_remote_copy(
            src_ref=gathered.at[far, BLOCKS - 1],
            dst_ref=roots.at[leaf],
            send_sem=root_send.at[k],
            recv_sem=root_recv.at[k],
            device_id=(leaf_peer(k), far),
            device_id_type=MESH,
        )
        copy.start()
        root_copies.append(copy)
    sib_copy(2, 1).start()

    for copy in halo:
        copy.wait()

    blank_row = lax.broadcasted_iota(jnp.int32, (FEATS, P_SIZE), 0)
    blank = jnp.where((blank_row >= 3) & (blank_row < 6), 1.0, 0.0).astype(BF)
    for where, first in ((0, 0), (N_LEAF - 1, LEAVES + HALO)):

        @pl.when(leaf == where)
        def _():
            for t in range(HALO):
                window[first + t, 0:RANK] = jnp.zeros((RANK, P_SIZE), BF)
                window[first + t, RANK : RANK + FEATS] = blank

    def turn(q, carry):
        block = jnp.concatenate(
            [target_feats[:, lanes(8 * q + t)] for t in range(8)], axis=0
        )
        block = block.astype(F32).T.astype(BF)
        for t in range(8):
            target_turned[8 * q + t] = block[:, t * FEATS : (t + 1) * FEATS]
        return carry

    lax.fori_loop(0, LEAVES // 8, turn, 0)

    def top_up():
        for copy in root_copies:
            copy.wait()
        h = [roots[g][:, :RANK] for g in range(N_LEAF)]
        for level in range(4):
            start = TOP_START[level]
            mapped = [
                jnp.dot(h[g], tops[start + g], preferred_element_type=F32)
                for g in range(len(h))
            ]
            h = [
                ((mapped[2 * g] + mapped[2 * g + 1]) * HALF_ROOT).astype(BF)
                for g in range(len(h) // 2)
            ]
        tops_in[far] = jnp.concatenate([h[0], h[0]], axis=1)

    def top_copy(k):
        block = tops_in.at[far]
        return pltpu.make_async_remote_copy(
            src_ref=block,
            dst_ref=block,
            send_sem=top_send.at[k],
            recv_sem=top_recv.at[k],
            device_id=(leaf, far_peer(k)),
            device_id_type=MESH,
        )

    def top_down():
        for k in range(1, N_FAR):
            top_copy(k).wait()
        load_root_blocks.wait()
        local = jnp.zeros((RANK, RANK), F32)
        for p in range(N_FAR):
            local = local + root_pattern[0, p].astype(F32) * jnp.dot(
                tops_in[p][:, :RANK], root_blocks[p], preferred_element_type=F32
            )
        for level in reversed(range(4)):
            e = tops[TOP_START[level] + lax.shift_right_logical(leaf, level)]
            local = lax.dot_general(
                local.astype(BF), e, (((1,), (1,)), ((), ())), preferred_element_type=F32
            )
        descent[...] = local

    def near_leaf(i, carry):
        target = target_turned[i]
        total = jnp.zeros((RANK, P_SIZE), F32)
        for q in range(NEAR // 2):
            near = [offsets[i, 2 * q + t] + (i + HALO) for t in range(2)]
            source = jnp.concatenate(
                [window[at, RANK : RANK + FEATS] for at in near], axis=1
            )
            x = jnp.concatenate([window[at, 0:RANK] for at in near], axis=1)
            inverse = lax.rsqrt(
                jnp.dot(target, source, preferred_element_type=F32).astype(BF)
            )
            total = total + lax.dot_general(
                x, inverse, (((1,), (1,)), ((), ())), preferred_element_type=F32
            )
        near_sum[:, lanes(i)] = total
        return carry

    def segment(step, carry):
        lax.fori_loop(
            step * LEAVES // STEPS, (step + 1) * LEAVES // STEPS, near_leaf, 0
        )
        for way in range(2):
            ring_copy(way, step).wait_recv()

            @pl.when(step + 2 < STEPS)
            def _():
                ring_copy(way, step + 2).start()

            sib_copy(way, step).start()

        @pl.when(step == 0)
        def _():
            top_up()
            for k in range(1, N_FAR):
                top_copy(k).start()

        @pl.when(step == 2)
        def _():
            top_down()

        return carry

    lax.fori_loop(0, STEPS, segment, 0)

    for step in range(STEPS):
        for way in range(2):
            ring_copy(way, step).wait_send()
            sib_copy(way, step).wait()
    for piece in range(2):
        sib_copy(2, piece).wait()
    load_coupling.wait()

    def gain(row, parity):
        block = row // 2
        parts = [
            gathered[pattern[row, k], block][:, parity * RANK : (parity + 1) * RANK]
            for k in range(KC)
        ]
        gains[row] = jnp.dot(
            jnp.concatenate(parts, axis=1),
            coupling[row].reshape(KC * RANK, RANK),
            preferred_element_type=F32,
        )

    def gain_pair(q, carry):
        gain(2 * q, 0)
        gain(2 * q + 1, 1)
        return carry

    lax.fori_loop(0, NODES // 2, gain_pair, 0, unroll=4)
    gain(NODES - 1, 0)

    def down(level, j):
        start = CHILD_START[level - 1]
        e = transfer[pl.ds(start + 2 * j, 2)].reshape(2 * RANK, RANK)
        return lax.dot_general(
            expansion[ROW_START[level] + j],
            e,
            (((1,), (1,)), ((), ())),
            preferred_element_type=F32,
        )

    expansion[NODES - 1] = (descent[...] + gains[NODES - 1]).astype(BF)

    def down_level(level):
        def node(j, carry):
            both = down(level, j)
            for t in range(2):
                row = ROW_START[level - 1] + 2 * j + t
                expansion[row] = (
                    both[:, t * RANK : (t + 1) * RANK] + gains[row]
                ).astype(BF)
            return carry

        count = LEAVES >> level
        lax.fori_loop(0, count, node, 0, unroll=min(count, 8))

    for level in range(6, 1, -1):
        down_level(level)

    factor = 1.0 / math.sqrt(NEAR * P_SIZE)

    def finish(j, carry):
        both = down(1, j).astype(BF)
        for t in range(2):
            at = lanes(2 * j + t)
            far_sum = jnp.dot(
                both[:, t * RANK : (t + 1) * RANK], basis[:, at], preferred_element_type=F32
            )
            out_vmem[:, at] = (near_sum[:, at] * factor + far_sum).astype(BF)
        return carry

    lax.fori_loop(0, PAIRS, finish, 0, unroll=4)
    store = pltpu.make_async_copy(out_vmem, out_hbm, load_sem.at[0])
    store.start()
    store.wait()


def local(
    right_sides,
    point_coords,
    near_offsets,
    leaf_basis,
    local_transfer,
    top_transfer,
    coupling_pattern,
    coupling_blocks,
    root_pattern,
    root_blocks,
):
    smem = pl.BlockSpec(memory_space=pltpu.SMEM)
    vmem = pl.BlockSpec(memory_space=pltpu.VMEM)
    hbm = pl.BlockSpec(memory_space=pl.ANY)
    points = LEAVES * P_SIZE
    dma = pltpu.SemaphoreType.DMA
    out = pl.pallas_call(
        kernel,
        name="h2_product",
        out_shape=jax.ShapeDtypeStruct((RANK, points), BF),
        in_specs=[smem, smem, smem, vmem, vmem, hbm, hbm, hbm, hbm, hbm],
        out_specs=hbm,
        scratch_shapes=[
            pltpu.VMEM((WINDOW, RANK + FEATS, P_SIZE), BF),
            pltpu.VMEM((FEATS, points), BF),
            pltpu.VMEM((LEAVES, P_SIZE, FEATS), BF),
            pltpu.VMEM((RANK, points), BF),
            pltpu.VMEM((2 * NODES, RANK, RANK), BF),
            pltpu.VMEM((NODES, KC, RANK, RANK), BF),
            pltpu.VMEM((N_FAR, RANK, RANK), BF),
            pltpu.VMEM((PAIRS, RANK, 2 * RANK), BF),
            pltpu.VMEM((N_FAR, BLOCKS, RANK, 2 * RANK), BF),
            pltpu.VMEM((N_LEAF, RANK, 2 * RANK), BF),
            pltpu.VMEM((N_FAR, RANK, 2 * RANK), BF),
            pltpu.VMEM((RANK, RANK), F32),
            pltpu.VMEM((NODES, RANK, RANK), F32),
            pltpu.VMEM((NODES, RANK, RANK), BF),
            pltpu.VMEM((RANK, points), F32),
            pltpu.VMEM((RANK, points), BF),
            dma((5,)),
            dma((LEAVES,)),
            dma((2,)),
            dma((2,)),
            dma((2, STEPS)),
            dma((2, STEPS)),
            dma((3, STEPS)),
            dma((3, STEPS)),
            dma((N_LEAF,)),
            dma((N_LEAF,)),
            dma((N_FAR,)),
            dma((N_FAR,)),
        ],
        compiler_params=pltpu.CompilerParams(
            collective_id=0, has_side_effects=True, vmem_limit_bytes=52 << 20
        ),
        cost_estimate=pl.CostEstimate(
            flops=4 << 30, bytes_accessed=16 << 20, transcendentals=25 << 20
        ),
    )(
        near_offsets[0],
        coupling_pattern[0],
        root_pattern,
        point_coords[0],
        top_transfer[0],
        right_sides[0],
        leaf_basis[0],
        local_transfer[0],
        coupling_blocks[0],
        root_blocks[0],
    )
    return out[None]


def solution(mesh):
    return jax.shard_map(
        local,
        mesh=mesh,
        in_specs=(
            P("far", None, "leaf"),
            P("far", None, "leaf"),
            P("far", "leaf", None),
            P("far", None, "leaf"),
            P("far", "leaf", None, None),
            P("far", None, None, None),
            P("far", "leaf", None),
            P("far", "leaf", None, None, None),
            P("far", None),
            P("far", None, None, None),
        ),
        out_specs=P("far", None, "leaf"),
        check_vma=False,
    )
```

```python
import functools
import math

import jax
import jax.numpy as jnp
from jax import lax
from jax.experimental import pallas as pl
from jax.experimental.pallas import tpu as pltpu
from jax.sharding import PartitionSpec as P

BF = jnp.bfloat16
F32 = jnp.float32
MESH = pl.DeviceIdType.MESH
HALO = 16
HALF_ROOT = 0.7071067811865476
SOFTEN = 0.0004
LEAVES = 64
WINDOW = LEAVES + 2 * HALO
P_SIZE = 128
RANK = 64
NEAR = 24
KC = 4
N_LEAF = 16
N_FAR = 16
PAIRS = LEAVES // 2
NODES = LEAVES - 1
BLOCKS = 32
PIECE = BLOCKS // 2
RING = N_FAR // 2
STEPS = 7
GROUP = 4
GROUPS = LEAVES // GROUP
FEATS = 16
CHILD_START = (0, 64, 96, 112, 120, 124)
ROW_START = (None, 0, 32, 48, 56, 60, 62)
TOP_START = (0, 16, 24, 28)


def lanes(index, count=1):
    return pl.ds(pl.multiple_of(index * P_SIZE, P_SIZE), count * P_SIZE)


def split3(value):
    high = value.astype(BF).astype(F32)
    rest = value - high
    middle = rest.astype(BF).astype(F32)
    return high, middle, rest - middle


def folded(square):
    return jnp.concatenate([square[: RANK // 2], square[RANK // 2 :]], axis=1)


def unfolded(block):
    return jnp.concatenate([block[:, :RANK], block[:, RANK:]], axis=0)


def stacked_rows(rows, width):
    at = lax.broadcasted_iota(jnp.int32, (FEATS, width), 0)
    out = jnp.zeros((FEATS, width), F32)
    for r, row in enumerate(rows):
        out = jnp.where(at == r, row, out)
    return out.astype(BF)


def kernel(
    offsets,
    pattern,
    root_pattern,
    coords,
    tops,
    x_hbm,
    basis_hbm,
    transfer_hbm,
    coupling_hbm,
    root_blocks_hbm,
    out_hbm,
    window,
    target_feats,
    halo_in,
    source_coords,
    basis,
    transfer,
    coupling,
    root_blocks,
    h0,
    gathered,
    roots,
    tops_in,
    descent,
    expansion,
    near_sum,
    out_vmem,
    load_sem,
    x_sem,
    halo_send,
    halo_recv,
    ring_send,
    ring_recv,
    sib_send,
    sib_recv,
    root_send,
    root_recv,
    top_send,
    top_recv,
):
    leaf = lax.axis_index("leaf")
    far = lax.axis_index("far")
    z = far // 2
    core = lax.rem(far, 2)
    sibling = z * 2 + (1 - core)

    def column(step):
        return lax.rem(z + RING + step, RING) * 2 + core

    def leaf_peer(k):
        return lax.rem(leaf + k + N_LEAF, N_LEAF)

    def far_peer(k):
        return lax.rem(far + k + N_FAR, N_FAR)

    barrier = pltpu.get_barrier_semaphore()
    for k in range(1, N_LEAF):
        pl.semaphore_signal(
            barrier, inc=1, device_id=(leaf_peer(k), far), device_id_type=MESH
        )
    for k in range(1, N_FAR):
        pl.semaphore_signal(
            barrier, inc=1, device_id=(leaf, far_peer(k)), device_id_type=MESH
        )

    def load_x(i):
        return pltpu.make_async_copy(
            x_hbm.at[:, lanes(i)], window.at[HALO + i, pl.ds(0, RANK)], x_sem.at[i]
        )

    def start_x(i, carry):
        load_x(i).start()
        return carry

    def wait_x(i, carry):
        load_x(i).wait()
        return carry

    lax.fori_loop(0, LEAVES, start_x, 0)
    load_basis = pltpu.make_async_copy(basis_hbm, basis, load_sem.at[1])
    load_basis.start()
    load_transfer = pltpu.make_async_copy(transfer_hbm, transfer, load_sem.at[2])
    load_transfer.start()
    load_coupling = pltpu.make_async_copy(coupling_hbm, coupling, load_sem.at[3])
    load_root_blocks = pltpu.make_async_copy(root_blocks_hbm, root_blocks, load_sem.at[4])
    load_coupling.start()
    load_root_blocks.start()

    chunk = 1024

    def make_feats(q, carry):
        at = pl.ds(pl.multiple_of(q * chunk, chunk), chunk)
        c = coords[:, at].astype(F32)
        rows = [c[r : r + 1] for r in range(3)]
        square = rows[0] * rows[0] + rows[1] * rows[1] + rows[2] * rows[2]
        one = jnp.ones_like(square)
        feats = stacked_rows([*rows, one, one, one, *split3(square)], chunk)
        for t in range(chunk // P_SIZE):
            window[HALO + q * (chunk // P_SIZE) + t, RANK : RANK + FEATS] = feats[
                :, t * P_SIZE : (t + 1) * P_SIZE
            ]
        target_feats[:, at] = stacked_rows(
            [*(-2.0 * row for row in rows), *split3(square + SOFTEN), one, one, one], chunk
        )
        return carry

    lax.fori_loop(0, LEAVES * P_SIZE // chunk, make_feats, 0)
    lax.fori_loop(0, LEAVES, wait_x, 0)
    pl.semaphore_wait(barrier, N_LEAF - 1 + N_FAR - 1)

    halo = []
    for way, src in enumerate((LEAVES, HALO)):
        copy = pltpu.make_async_remote_copy(
            src_ref=window.at[pl.ds(src, HALO)],
            dst_ref=halo_in.at[way],
            send_sem=halo_send.at[way],
            recv_sem=halo_recv.at[way],
            device_id=(leaf_peer(1 if way == 0 else -1), far),
            device_id_type=MESH,
        )
        copy.start()
        halo.append(copy)

    load_basis.wait()

    def leaf_pair(q, carry):
        parts = []
        for t in range(2):
            x = window[HALO + 2 * q + t, 0:RANK]
            b = basis[:, lanes(2 * q + t)]
            parts.append(
                lax.dot_general(
                    x, b, (((1,), (1,)), ((), ())), preferred_element_type=F32
                )
            )
        h0[q] = jnp.concatenate(parts, axis=1).astype(BF)
        return carry

    lax.fori_loop(0, PAIRS, leaf_pair, 0, unroll=8)
    load_transfer.wait()

    def piece_of(way, step):
        return 1 - lax.rem(step, 2) if way == 1 else lax.rem(step, 2)

    def ring_copy(way, step):
        piece = piece_of(way, step)
        behind = step // 2
        block = gathered.at[
            column(-behind if way == 0 else behind), pl.ds(piece * PIECE, PIECE)
        ]
        return pltpu.make_async_remote_copy(
            src_ref=block,
            dst_ref=block,
            send_sem=ring_send.at[way, step],
            recv_sem=ring_recv.at[way, step],
            device_id=(leaf, column(1 if way == 0 else -1)),
            device_id_type=MESH,
        )

    def sib_copy(way, step):
        piece = piece_of(way, step)
        behind = step // 2 + 1
        part = far if way == 2 else column(-behind if way == 0 else behind)
        block = gathered.at[part, pl.ds(piece * PIECE, PIECE)]
        return pltpu.make_async_remote_copy(
            src_ref=block,
            dst_ref=block,
            send_sem=sib_send.at[way, step],
            recv_sem=sib_recv.at[way, step],
            device_id=(leaf, sibling),
            device_id_type=MESH,
        )

    def up_level(level, sources):
        values = []
        for j, source in enumerate(sources):
            first = CHILD_START[level - 1] + 2 * j
            e = transfer[pl.ds(first, 2)].reshape(2 * RANK, RANK)
            values.append(jnp.dot(source, e, preferred_element_type=F32) * HALF_ROOT)
        return [
            jnp.concatenate(values[2 * q : 2 * q + 2], axis=1).astype(BF)
            for q in range(len(values) // 2)
        ]

    level1 = up_level(1, [h0[j] for j in range(PAIRS)])
    for q, block in enumerate(level1):
        gathered[far, q] = block
    ring_copy(0, 0).start()
    ring_copy(1, 1).start()
    sib_copy(2, 0).start()
    blocks = level1
    for level in range(2, 6):
        blocks = up_level(level, blocks)
        for q, block in enumerate(blocks):
            gathered[far, ROW_START[level] // 2 + q] = block
    e = transfer[pl.ds(CHILD_START[5], 2)].reshape(2 * RANK, RANK)
    root = (jnp.dot(blocks[0], e, preferred_element_type=F32) * HALF_ROOT).astype(BF)
    gathered[far, BLOCKS - 1] = jnp.concatenate([root, jnp.zeros_like(root)], axis=1)
    roots[leaf] = folded(root)
    ring_copy(0, 1).start()
    ring_copy(1, 0).start()
    root_copies = []
    for k in range(1, N_LEAF):
        copy = pltpu.make_async_remote_copy(
            src_ref=roots.at[leaf],
            dst_ref=roots.at[leaf],
            send_sem=root_send.at[k],
            recv_sem=root_recv.at[k],
            device_id=(leaf_peer(k), far),
            device_id_type=MESH,
        )
        copy.start()
        root_copies.append(copy)
    sib_copy(2, 1).start()

    def spread(q, carry):
        block = jnp.concatenate(
            [window[8 * q + t, RANK : RANK + FEATS] for t in range(8)], axis=0
        )
        block = block.astype(F32).T
        for t in range(8):
            for c in range(3):
                at = t * FEATS + c
                source_coords[8 * q + t, c] = jnp.broadcast_to(
                    block[:, at : at + 1], (P_SIZE, P_SIZE)
                )
        return carry

    lax.fori_loop(HALO // 8, (HALO + LEAVES) // 8, spread, 0)

    def halo_arrived():
        for copy in halo:
            copy.wait()
        row = lax.broadcasted_iota(jnp.int32, (RANK + FEATS, P_SIZE), 0)
        blank = jnp.where((row >= RANK + 3) & (row < RANK + 6), 1.0, 0.0).astype(BF)
        for way, (edge, first) in enumerate(((0, 0), (N_LEAF - 1, HALO + LEAVES))):

            @pl.when(leaf == edge)
            def _():
                for t in range(HALO):
                    window[first + t] = blank

            @pl.when(leaf != edge)
            def _():
                for t in range(HALO):
                    window[first + t] = halo_in[way, t]

            lax.fori_loop(first // 8, (first + HALO) // 8, spread, 0)


    def top_up():
        for copy in root_copies:
            copy.wait()
        h = [unfolded(roots[g]) for g in range(N_LEAF)]
        for level in range(4):
            start = TOP_START[level]
            mapped = [
                jnp.dot(h[g], tops[start + g], preferred_element_type=F32)
                for g in range(len(h))
            ]
            h = [
                ((mapped[2 * g] + mapped[2 * g + 1]) * HALF_ROOT).astype(BF)
                for g in range(len(h) // 2)
            ]
        tops_in[far] = folded(h[0])

    def top_copy(k):
        block = tops_in.at[far]
        return pltpu.make_async_remote_copy(
            src_ref=block,
            dst_ref=block,
            send_sem=top_send.at[k],
            recv_sem=top_recv.at[k],
            device_id=(leaf, far_peer(k)),
            device_id_type=MESH,
        )

    def top_down():
        for k in range(1, N_FAR):
            top_copy(k).wait()
        load_root_blocks.wait()
        local = jnp.zeros((RANK, RANK), F32)
        for p in range(N_FAR):
            local = local + root_pattern[0, p].astype(F32) * jnp.dot(
                unfolded(tops_in[p]), root_blocks[p], preferred_element_type=F32
            )
        for level in reversed(range(4)):
            e = tops[TOP_START[level] + lax.shift_right_logical(leaf, level)]
            local = lax.dot_general(
                local.astype(BF), e, (((1,), (1,)), ((), ())), preferred_element_type=F32
            )
        descent[...] = local

    def near_leaf(i):
        target = target_feats[:, lanes(i)].astype(F32).T.astype(BF)
        c = coords[:, lanes(i)].astype(F32)
        own = [
            jnp.broadcast_to(c[r : r + 1], (P_SIZE, P_SIZE)).astype(BF) for r in range(3)
        ]
        total = jnp.zeros((RANK, P_SIZE), F32)
        for q in range(NEAR // 2):
            near = [offsets[2 * q + t, i] + (i + HALO) for t in range(2)]
            x = jnp.concatenate([window[at, 0:RANK] for at in near], axis=1)
            if q % 3 == 0:
                source = jnp.concatenate(
                    [window[at, RANK : RANK + FEATS] for at in near], axis=1
                )
                square = jnp.dot(target, source, preferred_element_type=F32)
                total = total + lax.dot_general(
                    x,
                    lax.rsqrt(square.astype(BF)),
                    (((1,), (1,)), ((), ())),
                    preferred_element_type=F32,
                )
            else:
                inverse = []
                for at in near:
                    d = [source_coords[at, r].astype(BF) - own[r] for r in range(3)]
                    square = d[0] * d[0] + jnp.asarray(SOFTEN, BF)
                    square = square + d[1] * d[1]
                    square = square + d[2] * d[2]
                    inverse.append(lax.rsqrt(square))
                total = total + jnp.dot(
                    x, jnp.concatenate(inverse, axis=0), preferred_element_type=F32
                )
        return total

    def near_group(step, carry):
        p = lax.rem(step + HALO // GROUP, GROUPS)
        for t in range(GROUP):
            near_sum[:, lanes(GROUP * p + t)] = near_leaf(GROUP * p + t)
        return carry

    def segment(step, carry):
        lax.fori_loop(
            step * GROUPS // STEPS, (step + 1) * GROUPS // STEPS, near_group, 0
        )
        for way in range(2):
            ring_copy(way, step).wait_recv()

            @pl.when(step + 2 < STEPS)
            def _():
                ring_copy(way, step + 2).start()

            sib_copy(way, step).start()

        @pl.when(step == 0)
        def _():
            top_up()
            for k in range(1, N_FAR):
                top_copy(k).start()

        @pl.when(step == 2)
        def _():
            halo_arrived()

        @pl.when(step == 3)
        def _():
            top_down()

        return carry

    lax.fori_loop(0, STEPS, segment, 0)

    for step in range(STEPS):
        for way in range(2):
            ring_copy(way, step).wait_send()
            sib_copy(way, step).wait()
    for piece in range(2):
        sib_copy(2, piece).wait()
    load_coupling.wait()

    def gain(row):
        half = slice((row % 2) * RANK, (row % 2 + 1) * RANK)
        parts = [gathered[pattern[k, row], row // 2][:, half] for k in range(KC)]
        return jnp.dot(
            jnp.concatenate(parts, axis=1),
            coupling[row].reshape(KC * RANK, RANK),
            preferred_element_type=F32,
        )

    def down(level, j, value):
        start = CHILD_START[level - 1]
        e = transfer[pl.ds(start + 2 * j, 2)].reshape(2 * RANK, RANK)
        both = lax.dot_general(
            value, e, (((1,), (1,)), ((), ())), preferred_element_type=F32
        )
        return both[:, :RANK], both[:, RANK:]

    values = [(descent[...] + gain(NODES - 1)).astype(BF)]
    for level in range(6, 1, -1):
        children = []
        for j, value in enumerate(values):
            children += down(level, j, value)
        values = [
            (child + gain(ROW_START[level - 1] + j)).astype(BF)
            for j, child in enumerate(children)
        ]
    for j, value in enumerate(values):
        expansion[j] = value

    factor = 1.0 / math.sqrt(NEAR * P_SIZE)

    def finish(j, carry):
        both = down(1, j, expansion[j])
        for t in range(2):
            at = lanes(2 * j + t)
            far_sum = jnp.dot(
                both[t].astype(BF), basis[:, at], preferred_element_type=F32
            )
            out_vmem[:, at] = (near_sum[:, at] * factor + far_sum).astype(BF)
        return carry

    lax.fori_loop(0, PAIRS, finish, 0, unroll=8)
    store = pltpu.make_async_copy(out_vmem, out_hbm, load_sem.at[0])
    store.start()
    store.wait()


def local(
    right_sides,
    point_coords,
    near_offsets,
    leaf_basis,
    local_transfer,
    top_transfer,
    coupling_pattern,
    coupling_blocks,
    root_pattern,
    root_blocks,
):
    smem = pl.BlockSpec(memory_space=pltpu.SMEM)
    vmem = pl.BlockSpec(memory_space=pltpu.VMEM)
    hbm = pl.BlockSpec(memory_space=pl.ANY)
    points = LEAVES * P_SIZE
    dma = pltpu.SemaphoreType.DMA
    out = pl.pallas_call(
        kernel,
        name="h2_product",
        out_shape=jax.ShapeDtypeStruct((RANK, points), BF),
        in_specs=[smem, smem, smem, vmem, vmem, hbm, hbm, hbm, hbm, hbm],
        out_specs=hbm,
        scratch_shapes=[
            pltpu.VMEM((WINDOW, RANK + FEATS, P_SIZE), BF),
            pltpu.VMEM((FEATS, points), BF),
            pltpu.VMEM((2, HALO, RANK + FEATS, P_SIZE), BF),
            pltpu.VMEM((WINDOW, 3, P_SIZE, P_SIZE), F32),
            pltpu.VMEM((RANK, points), BF),
            pltpu.VMEM((2 * NODES, RANK, RANK), BF),
            pltpu.VMEM((NODES, KC, RANK, RANK), BF),
            pltpu.VMEM((N_FAR, RANK, RANK), BF),
            pltpu.VMEM((PAIRS, RANK, 2 * RANK), BF),
            pltpu.VMEM((N_FAR, BLOCKS, RANK, 2 * RANK), BF),
            pltpu.VMEM((N_LEAF, RANK // 2, 2 * RANK), BF),
            pltpu.VMEM((N_FAR, RANK // 2, 2 * RANK), BF),
            pltpu.VMEM((RANK, RANK), F32),
            pltpu.VMEM((PAIRS, RANK, RANK), BF),
            pltpu.VMEM((RANK, points), F32),
            pltpu.VMEM((RANK, points), BF),
            dma((5,)),
            dma((LEAVES,)),
            dma((2,)),
            dma((2,)),
            dma((2, STEPS)),
            dma((2, STEPS)),
            dma((3, STEPS)),
            dma((3, STEPS)),
            dma((N_LEAF,)),
            dma((N_LEAF,)),
            dma((N_FAR,)),
            dma((N_FAR,)),
        ],
        compiler_params=pltpu.CompilerParams(
            collective_id=0, has_side_effects=True, vmem_limit_bytes=62 << 20
        ),
        cost_estimate=pl.CostEstimate(
            flops=4 << 30, bytes_accessed=16 << 20, transcendentals=25 << 20
        ),
    )(
        near_offsets[0].T,
        coupling_pattern[0].T,
        root_pattern,
        point_coords[0],
        top_transfer[0],
        right_sides[0],
        leaf_basis[0],
        local_transfer[0],
        coupling_blocks[0],
        root_blocks[0],
    )
    return out[None]


def solution(mesh):
    return jax.shard_map(
        local,
        mesh=mesh,
        in_specs=(
            P("far", None, "leaf"),
            P("far", None, "leaf"),
            P("far", "leaf", None),
            P("far", None, "leaf"),
            P("far", "leaf", None, None),
            P("far", None, None, None),
            P("far", "leaf", None),
            P("far", "leaf", None, None, None),
            P("far", None),
            P("far", None, None, None),
        ),
        out_specs=P("far", None, "leaf"),
        check_vma=False,
    )
```

```python
import functools
import math

import jax
import jax.numpy as jnp
from jax import lax
from jax.experimental import pallas as pl
from jax.experimental.pallas import tpu as pltpu
from jax.sharding import PartitionSpec as P

BF = jnp.bfloat16
F32 = jnp.float32
MESH = pl.DeviceIdType.MESH
HALO = 16
HALF_ROOT = 0.7071067811865476
SOFTEN = 0.0004
LEAVES = 64
WINDOW = LEAVES + 2 * HALO
P_SIZE = 128
RANK = 64
NEAR = 24
KC = 4
N_LEAF = 16
N_FAR = 16
PAIRS = LEAVES // 2
NODES = LEAVES - 1
PIECE = 16
RING = N_FAR // 2
EVENTS = 10
HALF_PIECE = PIECE // 2
GROUP = 4
GROUPS = LEAVES // GROUP
FEATS = 16
ROUTE = (
    (0, 2, 1),
    (1, 2, 1),
    (0, 0, 2),
    (1, 2, 2),
    (0, 1, 2),
    (1, 2, 3),
    (0, 0, 3),
    (1, 0, 4),
    (0, 1, 3),
    (0, 0, 4),
)
NEXT = {0: (2,), 1: (3, 4), 3: (5, 6), 5: (7, 8), 6: (9,)}
AFTER_GROUP = {1: (0,), 3: (1,), 4: (2,), 7: (3,), 8: (4,), 11: (5,), 12: (6,), 15: (7,)}
CHILD_START = (0, 64, 96, 112, 120, 124)
ROW_START = (None, 0, 32, 48, 56, 60, 62)
TOP_START = (0, 16, 24, 28)


def lanes(index, count=1):
    return pl.ds(pl.multiple_of(index * P_SIZE, P_SIZE), count * P_SIZE)


def split3(value):
    high = value.astype(BF).astype(F32)
    rest = value - high
    middle = rest.astype(BF).astype(F32)
    return high, middle, rest - middle


def folded(square):
    return jnp.concatenate([square[: RANK // 2], square[RANK // 2 :]], axis=1)


def unfolded(block):
    return jnp.concatenate([block[:, :RANK], block[:, RANK:]], axis=0)


def stacked_rows(rows, width):
    at = lax.broadcasted_iota(jnp.int32, (FEATS, width), 0)
    out = jnp.zeros((FEATS, width), F32)
    for r, row in enumerate(rows):
        out = jnp.where(at == r, row, out)
    return out.astype(BF)


def kernel(
    offsets,
    pattern,
    root_pattern,
    coords,
    tops,
    x_hbm,
    basis_hbm,
    transfer_hbm,
    coupling_hbm,
    root_blocks_hbm,
    out_hbm,
    window,
    target_feats,
    halo_in,
    source_coords,
    basis,
    transfer,
    coupling,
    root_blocks,
    h0,
    level1_in,
    upper_in,
    roots,
    tops_in,
    descent,
    expansion,
    near_sum,
    out_vmem,
    load_sem,
    x_sem,
    halo_send,
    halo_recv,
    ring_send,
    ring_recv,
    sib_send,
    sib_recv,
    root_send,
    root_recv,
    top_send,
    top_recv,
):
    leaf = lax.axis_index("leaf")
    far = lax.axis_index("far")
    z = far // 2
    core = lax.rem(far, 2)
    sibling = z * 2 + (1 - core)

    def column(step):
        return lax.rem(z + RING + step, RING) * 2 + core

    def leaf_peer(k):
        return lax.rem(leaf + k + N_LEAF, N_LEAF)

    def far_peer(k):
        return lax.rem(far + k + N_FAR, N_FAR)

    barrier = pltpu.get_barrier_semaphore()
    for k in range(1, N_LEAF):
        pl.semaphore_signal(
            barrier, inc=1, device_id=(leaf_peer(k), far), device_id_type=MESH
        )
    for k in range(1, N_FAR):
        pl.semaphore_signal(
            barrier, inc=1, device_id=(leaf, far_peer(k)), device_id_type=MESH
        )

    def load_x(i):
        return pltpu.make_async_copy(
            x_hbm.at[:, lanes(i)], window.at[HALO + i, pl.ds(0, RANK)], x_sem.at[i]
        )

    def start_x(i, carry):
        load_x(i).start()
        return carry

    def wait_x(i, carry):
        load_x(i).wait()
        return carry

    lax.fori_loop(0, LEAVES, start_x, 0)
    load_basis = pltpu.make_async_copy(basis_hbm, basis, load_sem.at[1])
    load_basis.start()
    load_transfer = pltpu.make_async_copy(transfer_hbm, transfer, load_sem.at[2])
    load_transfer.start()
    load_coupling = pltpu.make_async_copy(coupling_hbm, coupling, load_sem.at[3])
    load_root_blocks = pltpu.make_async_copy(root_blocks_hbm, root_blocks, load_sem.at[4])
    lax.fori_loop(0, LEAVES, wait_x, 0)
    load_basis.wait()

    def leaf_pair(q, carry):
        parts = []
        for t in range(2):
            x = window[HALO + 2 * q + t, 0:RANK]
            b = basis[:, lanes(2 * q + t)]
            parts.append(
                lax.dot_general(
                    x, b, (((1,), (1,)), ((), ())), preferred_element_type=F32
                )
            )
        h0[q] = jnp.concatenate(parts, axis=1).astype(BF)
        return carry

    lax.fori_loop(0, PAIRS, leaf_pair, 0, unroll=8)
    load_transfer.wait()

    def route(way, event):
        upper, part, distance = ROUTE[event]
        first = 0 if part == 2 else HALF_PIECE * (part ^ way)
        count = PIECE if part == 2 else HALF_PIECE
        return (upper_in if upper else level1_in), pl.ds(first, count), distance

    def ring_copy(way, event):
        ref, span, distance = route(way, event)
        behind = distance - 1
        block = ref.at[column(-behind if way == 0 else behind), span]
        return pltpu.make_async_remote_copy(
            src_ref=block,
            dst_ref=block,
            send_sem=ring_send.at[way, event],
            recv_sem=ring_recv.at[way, event],
            device_id=(leaf, column(1 if way == 0 else -1)),
            device_id_type=MESH,
        )

    def sib_copy(way, event):
        if way == 2:
            block = (upper_in if event else level1_in).at[far]
        else:
            ref, span, distance = route(way, event)
            block = ref.at[column(-distance if way == 0 else distance), span]
        return pltpu.make_async_remote_copy(
            src_ref=block,
            dst_ref=block,
            send_sem=sib_send.at[way, event],
            recv_sem=sib_recv.at[way, event],
            device_id=(leaf, sibling),
            device_id_type=MESH,
        )

    def arrived(event):
        for way in range(2):
            ring_copy(way, event).wait_recv()
            for later in NEXT.get(event, ()):
                ring_copy(way, later).start()
            sib_copy(way, event).start()

    def up_level(level, sources):
        values = []
        for j, source in enumerate(sources):
            first = CHILD_START[level - 1] + 2 * j
            e = transfer[pl.ds(first, 2)].reshape(2 * RANK, RANK)
            values.append(jnp.dot(source, e, preferred_element_type=F32) * HALF_ROOT)
        return [
            jnp.concatenate(values[2 * q : 2 * q + 2], axis=1).astype(BF)
            for q in range(len(values) // 2)
        ]

    level1 = up_level(1, [h0[j] for j in range(PAIRS)])
    for q, block in enumerate(level1):
        level1_in[far, q] = block
    pl.semaphore_wait(barrier, N_LEAF - 1 + N_FAR - 1)
    ring_copy(0, 0).start()
    ring_copy(1, 0).start()
    sib_copy(2, 0).start()
    blocks = level1
    for level in range(2, 6):
        blocks = up_level(level, blocks)
        for q, block in enumerate(blocks):
            upper_in[far, ROW_START[level] // 2 - PIECE + q] = block
    e = transfer[pl.ds(CHILD_START[5], 2)].reshape(2 * RANK, RANK)
    root = (jnp.dot(blocks[0], e, preferred_element_type=F32) * HALF_ROOT).astype(BF)
    upper_in[far, PIECE - 1] = jnp.concatenate([root, jnp.zeros_like(root)], axis=1)
    roots[leaf] = folded(root)
    ring_copy(0, 1).start()
    ring_copy(1, 1).start()
    root_copies = []
    for k in range(1, N_LEAF):
        copy = pltpu.make_async_remote_copy(
            src_ref=roots.at[leaf],
            dst_ref=roots.at[leaf],
            send_sem=root_send.at[k],
            recv_sem=root_recv.at[k],
            device_id=(leaf_peer(k), far),
            device_id_type=MESH,
        )
        copy.start()
        root_copies.append(copy)
    sib_copy(2, 1).start()

    load_coupling.start()
    load_root_blocks.start()

    chunk = 1024

    def make_feats(q, carry):
        at = pl.ds(pl.multiple_of(q * chunk, chunk), chunk)
        c = coords[:, at].astype(F32)
        rows = [c[r : r + 1] for r in range(3)]
        square = rows[0] * rows[0] + rows[1] * rows[1] + rows[2] * rows[2]
        one = jnp.ones_like(square)
        feats = stacked_rows([*rows, one, one, one, *split3(square)], chunk)
        for t in range(chunk // P_SIZE):
            window[HALO + q * (chunk // P_SIZE) + t, RANK : RANK + FEATS] = feats[
                :, t * P_SIZE : (t + 1) * P_SIZE
            ]
        target_feats[:, at] = stacked_rows(
            [*(-2.0 * row for row in rows), *split3(square + SOFTEN), one, one, one], chunk
        )
        return carry

    lax.fori_loop(0, LEAVES * P_SIZE // chunk, make_feats, 0)

    halo = []
    for way, src in enumerate((LEAVES, HALO)):
        copy = pltpu.make_async_remote_copy(
            src_ref=window.at[pl.ds(src, HALO)],
            dst_ref=halo_in.at[way],
            send_sem=halo_send.at[way],
            recv_sem=halo_recv.at[way],
            device_id=(leaf_peer(1 if way == 0 else -1), far),
            device_id_type=MESH,
        )
        copy.start()
        halo.append(copy)

    def spread(q, carry):
        block = jnp.concatenate(
            [window[8 * q + t, RANK : RANK + FEATS] for t in range(8)], axis=0
        )
        block = block.astype(F32).T
        for t in range(8):
            for c in range(3):
                at = t * FEATS + c
                source_coords[8 * q + t, c] = jnp.broadcast_to(
                    block[:, at : at + 1], (P_SIZE, P_SIZE)
                )
        return carry

    lax.fori_loop(HALO // 8, (HALO + LEAVES) // 8, spread, 0)

    def halo_arrived():
        for copy in halo:
            copy.wait()
        row = lax.broadcasted_iota(jnp.int32, (RANK + FEATS, P_SIZE), 0)
        blank = jnp.where((row >= RANK + 3) & (row < RANK + 6), 1.0, 0.0).astype(BF)
        for way, (edge, first) in enumerate(((0, 0), (N_LEAF - 1, HALO + LEAVES))):

            @pl.when(leaf == edge)
            def _():
                for t in range(HALO):
                    window[first + t] = blank

            @pl.when(leaf != edge)
            def _():
                for t in range(HALO):
                    window[first + t] = halo_in[way, t]

            lax.fori_loop(first // 8, (first + HALO) // 8, spread, 0)


    def top_up():
        for copy in root_copies:
            copy.wait()
        h = [unfolded(roots[g]) for g in range(N_LEAF)]
        for level in range(4):
            start = TOP_START[level]
            mapped = [
                jnp.dot(h[g], tops[start + g], preferred_element_type=F32)
                for g in range(len(h))
            ]
            h = [
                ((mapped[2 * g] + mapped[2 * g + 1]) * HALF_ROOT).astype(BF)
                for g in range(len(h) // 2)
            ]
        tops_in[far] = folded(h[0])

    def top_copy(k):
        block = tops_in.at[far]
        return pltpu.make_async_remote_copy(
            src_ref=block,
            dst_ref=block,
            send_sem=top_send.at[k],
            recv_sem=top_recv.at[k],
            device_id=(leaf, far_peer(k)),
            device_id_type=MESH,
        )

    def top_down():
        for k in range(1, N_FAR):
            top_copy(k).wait()
        load_root_blocks.wait()
        local = jnp.zeros((RANK, RANK), F32)
        for p in range(N_FAR):
            local = local + root_pattern[0, p].astype(F32) * jnp.dot(
                unfolded(tops_in[p]), root_blocks[p], preferred_element_type=F32
            )
        for level in reversed(range(4)):
            e = tops[TOP_START[level] + lax.shift_right_logical(leaf, level)]
            local = lax.dot_general(
                local.astype(BF), e, (((1,), (1,)), ((), ())), preferred_element_type=F32
            )
        descent[...] = local

    def near_leaf(i):
        target = target_feats[:, lanes(i)].astype(F32).T.astype(BF)
        c = coords[:, lanes(i)].astype(F32)
        own = [
            jnp.broadcast_to(c[r : r + 1], (P_SIZE, P_SIZE)).astype(BF) for r in range(3)
        ]
        total = jnp.zeros((RANK, P_SIZE), F32)
        for q in range(NEAR // 2):
            near = [offsets[2 * q + t, i] + (i + HALO) for t in range(2)]
            x = jnp.concatenate([window[at, 0:RANK] for at in near], axis=1)
            if q % 3 == 0:
                source = jnp.concatenate(
                    [window[at, RANK : RANK + FEATS] for at in near], axis=1
                )
                square = jnp.dot(target, source, preferred_element_type=F32)
                total = total + lax.dot_general(
                    x,
                    lax.rsqrt(square.astype(BF)),
                    (((1,), (1,)), ((), ())),
                    preferred_element_type=F32,
                )
            else:
                inverse = []
                for at in near:
                    d = [source_coords[at, r].astype(BF) - own[r] for r in range(3)]
                    square = d[0] * d[0] + jnp.asarray(SOFTEN, BF)
                    square = square + d[1] * d[1]
                    square = square + d[2] * d[2]
                    inverse.append(lax.rsqrt(square))
                total = total + jnp.dot(
                    x, jnp.concatenate(inverse, axis=0), preferred_element_type=F32
                )
        return total

    def near_group(step, carry):
        p = lax.rem(step + HALO // GROUP, GROUPS)
        for t in range(GROUP):
            near_sum[:, lanes(GROUP * p + t)] = near_leaf(GROUP * p + t)
        for group, events in AFTER_GROUP.items():

            @pl.when(step == group)
            def _():
                for event in events:
                    arrived(event)

        @pl.when(step == 2)
        def _():
            top_up()
            for k in range(1, N_FAR):
                top_copy(k).start()

        @pl.when(step == 6)
        def _():
            halo_arrived()

        @pl.when(step == 9)
        def _():
            top_down()

        return carry

    lax.fori_loop(0, GROUPS, near_group, 0)
    load_coupling.wait()

    def gain(row, parity, upper):
        half = slice(parity * RANK, (parity + 1) * RANK)
        ref, block = (upper_in, row // 2 - PIECE) if upper else (level1_in, row // 2)
        parts = [ref[pattern[k, row], block][:, half] for k in range(KC)]
        return jnp.dot(
            jnp.concatenate(parts, axis=1),
            coupling[row].reshape(KC * RANK, RANK),
            preferred_element_type=F32,
        )

    def others(upper):
        events = [(2, upper)]
        for event in range(EVENTS):
            if ROUTE[event][0] == upper:
                events += [(0, event), (1, event)]
        return events

    for way, event in others(1):
        sib_copy(way, event).wait_recv()

    def down(level, j, value):
        start = CHILD_START[level - 1]
        e = transfer[pl.ds(start + 2 * j, 2)].reshape(2 * RANK, RANK)
        both = lax.dot_general(
            value, e, (((1,), (1,)), ((), ())), preferred_element_type=F32
        )
        return both[:, :RANK], both[:, RANK:]

    values = [(descent[...] + gain(NODES - 1, 0, True)).astype(BF)]
    for level in range(6, 1, -1):
        children = []
        for j, value in enumerate(values):
            children += down(level, j, value)
        if level > 2:
            start = ROW_START[level - 1]
            values = [
                (child + gain(start + j, j % 2, True)).astype(BF)
                for j, child in enumerate(children)
            ]
    for j, child in enumerate(children):
        expansion[j] = child

    for event in (8, 9):
        arrived(event)
    for way, event in others(0):
        sib_copy(way, event).wait_recv()

    factor = 1.0 / math.sqrt(NEAR * P_SIZE)

    def finish(q, carry):
        for parity in range(2):
            j = 2 * q + parity
            value = (expansion[j] + gain(j, parity, False)).astype(BF)
            both = down(1, j, value)
            for t in range(2):
                at = lanes(2 * j + t)
                far_sum = jnp.dot(
                    both[t].astype(BF), basis[:, at], preferred_element_type=F32
                )
                out_vmem[:, at] = (near_sum[:, at] * factor + far_sum).astype(BF)
        return carry

    lax.fori_loop(0, PAIRS // 2, finish, 0, unroll=8)
    store = pltpu.make_async_copy(out_vmem, out_hbm, load_sem.at[0])
    store.start()
    for event in range(EVENTS):
        for way in range(2):
            ring_copy(way, event).wait_send()
    for way, event in others(0) + others(1):
        sib_copy(way, event).wait_send()
    store.wait()


def local(
    right_sides,
    point_coords,
    near_offsets,
    leaf_basis,
    local_transfer,
    top_transfer,
    coupling_pattern,
    coupling_blocks,
    root_pattern,
    root_blocks,
):
    smem = pl.BlockSpec(memory_space=pltpu.SMEM)
    vmem = pl.BlockSpec(memory_space=pltpu.VMEM)
    hbm = pl.BlockSpec(memory_space=pl.ANY)
    points = LEAVES * P_SIZE
    dma = pltpu.SemaphoreType.DMA
    out = pl.pallas_call(
        kernel,
        name="h2_product",
        out_shape=jax.ShapeDtypeStruct((RANK, points), BF),
        in_specs=[smem, smem, smem, vmem, vmem, hbm, hbm, hbm, hbm, hbm],
        out_specs=hbm,
        scratch_shapes=[
            pltpu.VMEM((WINDOW, RANK + FEATS, P_SIZE), BF),
            pltpu.VMEM((FEATS, points), BF),
            pltpu.VMEM((2, HALO, RANK + FEATS, P_SIZE), BF),
            pltpu.VMEM((WINDOW, 3, P_SIZE, P_SIZE), F32),
            pltpu.VMEM((RANK, points), BF),
            pltpu.VMEM((2 * NODES, RANK, RANK), BF),
            pltpu.VMEM((NODES, KC, RANK, RANK), BF),
            pltpu.VMEM((N_FAR, RANK, RANK), BF),
            pltpu.VMEM((PAIRS, RANK, 2 * RANK), BF),
            pltpu.VMEM((N_FAR, PIECE, RANK, 2 * RANK), BF),
            pltpu.VMEM((N_FAR, PIECE, RANK, 2 * RANK), BF),
            pltpu.VMEM((N_LEAF, RANK // 2, 2 * RANK), BF),
            pltpu.VMEM((N_FAR, RANK // 2, 2 * RANK), BF),
            pltpu.VMEM((RANK, RANK), F32),
            pltpu.VMEM((PAIRS, RANK, RANK), F32),
            pltpu.VMEM((RANK, points), F32),
            pltpu.VMEM((RANK, points), BF),
            dma((5,)),
            dma((LEAVES,)),
            dma((2,)),
            dma((2,)),
            dma((2, EVENTS)),
            dma((2, EVENTS)),
            dma((3, EVENTS)),
            dma((3, EVENTS)),
            dma((N_LEAF,)),
            dma((N_LEAF,)),
            dma((N_FAR,)),
            dma((N_FAR,)),
        ],
        compiler_params=pltpu.CompilerParams(
            collective_id=0, has_side_effects=True, vmem_limit_bytes=62 << 20
        ),
        cost_estimate=pl.CostEstimate(
            flops=4 << 30, bytes_accessed=16 << 20, transcendentals=25 << 20
        ),
    )(
        near_offsets[0].T,
        coupling_pattern[0].T,
        root_pattern,
        point_coords[0],
        top_transfer[0],
        right_sides[0],
        leaf_basis[0],
        local_transfer[0],
        coupling_blocks[0],
        root_blocks[0],
    )
    return out[None]


def solution(mesh):
    return jax.shard_map(
        local,
        mesh=mesh,
        in_specs=(
            P("far", None, "leaf"),
            P("far", None, "leaf"),
            P("far", "leaf", None),
            P("far", None, "leaf"),
            P("far", "leaf", None, None),
            P("far", None, None, None),
            P("far", "leaf", None),
            P("far", "leaf", None, None, None),
            P("far", None),
            P("far", None, None, None),
        ),
        out_specs=P("far", None, "leaf"),
        check_vma=False,
    )
```

```python
import functools
import math

import jax
import jax.numpy as jnp
from jax import lax
from jax.experimental import pallas as pl
from jax.experimental.pallas import tpu as pltpu
from jax.sharding import PartitionSpec as P

BF = jnp.bfloat16
F32 = jnp.float32
MESH = pl.DeviceIdType.MESH
HALO = 16
HALF_ROOT = 0.7071067811865476
SOFTEN = 0.0004
LEAVES = 64
WINDOW = LEAVES + 2 * HALO
P_SIZE = 128
RANK = 64
NEAR = 24
KC = 4
N_LEAF = 16
N_FAR = 16
PAIRS = LEAVES // 2
NODES = LEAVES - 1
PIECE = 16
RING = N_FAR // 2
EVENTS = 10
HALF_PIECE = PIECE // 2
GROUP = 4
GROUPS = LEAVES // GROUP
FEATS = 16
ROUTE = (
    (0, 2, 1),
    (1, 2, 1),
    (0, 0, 2),
    (1, 2, 2),
    (0, 1, 2),
    (1, 2, 3),
    (0, 0, 3),
    (1, 0, 4),
    (0, 1, 3),
    (0, 0, 4),
)
NEXT = {0: (2,), 1: (3, 4), 3: (5, 6), 5: (7, 8), 6: (9,)}
AFTER_GROUP = {1: (0,), 3: (1,), 4: (2,), 7: (3,), 8: (4,), 11: (5,), 12: (6,), 15: (7,)}
CHILD_START = (0, 64, 96, 112, 120, 124)
ROW_START = (None, 0, 32, 48, 56, 60, 62)
TOP_START = (0, 16, 24, 28)


def lanes(index, count=1):
    return pl.ds(pl.multiple_of(index * P_SIZE, P_SIZE), count * P_SIZE)


def split3(value):
    high = value.astype(BF).astype(F32)
    rest = value - high
    middle = rest.astype(BF).astype(F32)
    return high, middle, rest - middle


def folded(square):
    return jnp.concatenate([square[: RANK // 2], square[RANK // 2 :]], axis=1)


def unfolded(block):
    return jnp.concatenate([block[:, :RANK], block[:, RANK:]], axis=0)


def stacked_rows(rows, width):
    at = lax.broadcasted_iota(jnp.int32, (FEATS, width), 0)
    out = jnp.zeros((FEATS, width), F32)
    for r, row in enumerate(rows):
        out = jnp.where(at == r, row, out)
    return out.astype(BF)


def kernel(
    offsets,
    pattern,
    root_pattern,
    coords,
    tops,
    x_hbm,
    basis_hbm,
    transfer_hbm,
    coupling_hbm,
    root_blocks_hbm,
    out_hbm,
    window,
    target_feats,
    halo_in,
    source_coords,
    basis,
    transfer,
    coupling,
    root_blocks,
    h0,
    level1_in,
    upper_in,
    roots,
    tops_in,
    descent,
    expansion,
    near_sum,
    out_vmem,
    load_sem,
    x_sem,
    halo_send,
    halo_recv,
    ring_send,
    ring_recv,
    sib_send,
    sib_recv,
    root_send,
    root_recv,
    top_send,
    top_recv,
):
    leaf = lax.axis_index("leaf")
    far = lax.axis_index("far")
    z = far // 2
    core = lax.rem(far, 2)
    sibling = z * 2 + (1 - core)

    def column(step):
        return lax.rem(z + RING + step, RING) * 2 + core

    def leaf_peer(k):
        return lax.rem(leaf + k + N_LEAF, N_LEAF)

    def far_peer(k):
        return lax.rem(far + k + N_FAR, N_FAR)

    load_rows = pltpu.make_async_copy(x_hbm, out_vmem, load_sem.at[0])
    load_rows.start()
    load_basis = pltpu.make_async_copy(basis_hbm, basis, load_sem.at[1])
    load_basis.start()
    load_transfer = pltpu.make_async_copy(transfer_hbm, transfer, load_sem.at[2])
    load_transfer.start()

    barrier = pltpu.get_barrier_semaphore()
    for k in range(1, N_LEAF):
        pl.semaphore_signal(
            barrier, inc=1, device_id=(leaf_peer(k), far), device_id_type=MESH
        )
    for k in range(1, N_FAR):
        pl.semaphore_signal(
            barrier, inc=1, device_id=(leaf, far_peer(k)), device_id_type=MESH
        )

    def load_x(i):
        return pltpu.make_async_copy(
            x_hbm.at[:, lanes(i)], window.at[HALO + i, pl.ds(0, RANK)], x_sem.at[i]
        )

    def start_x(i, carry):
        load_x(i).start()
        return carry

    def wait_x(i, carry):
        load_x(i).wait()
        return carry

    load_coupling = pltpu.make_async_copy(coupling_hbm, coupling, load_sem.at[3])
    load_root_blocks = pltpu.make_async_copy(root_blocks_hbm, root_blocks, load_sem.at[4])
    load_rows.wait()
    load_basis.wait()

    def leaf_pair(q, carry):
        parts = []
        for t in range(2):
            x = out_vmem[:, lanes(2 * q + t)]
            b = basis[:, lanes(2 * q + t)]
            parts.append(
                lax.dot_general(
                    x, b, (((1,), (1,)), ((), ())), preferred_element_type=F32
                )
            )
        h0[q] = jnp.concatenate(parts, axis=1).astype(BF)
        return carry

    lax.fori_loop(0, PAIRS, leaf_pair, 0, unroll=8)
    load_transfer.wait()

    def route(way, event):
        upper, part, distance = ROUTE[event]
        first = 0 if part == 2 else HALF_PIECE * (part ^ way)
        count = PIECE if part == 2 else HALF_PIECE
        return (upper_in if upper else level1_in), pl.ds(first, count), distance

    def ring_copy(way, event):
        ref, span, distance = route(way, event)
        behind = distance - 1
        block = ref.at[column(-behind if way == 0 else behind), span]
        return pltpu.make_async_remote_copy(
            src_ref=block,
            dst_ref=block,
            send_sem=ring_send.at[way, event],
            recv_sem=ring_recv.at[way, event],
            device_id=(leaf, column(1 if way == 0 else -1)),
            device_id_type=MESH,
        )

    def sib_copy(way, event):
        if way == 2:
            block = (upper_in if event else level1_in).at[far]
        else:
            ref, span, distance = route(way, event)
            block = ref.at[column(-distance if way == 0 else distance), span]
        return pltpu.make_async_remote_copy(
            src_ref=block,
            dst_ref=block,
            send_sem=sib_send.at[way, event],
            recv_sem=sib_recv.at[way, event],
            device_id=(leaf, sibling),
            device_id_type=MESH,
        )

    def arrived(event):
        for way in range(2):
            ring_copy(way, event).wait_recv()
            for later in NEXT.get(event, ()):
                ring_copy(way, later).start()
            sib_copy(way, event).start()

    def up_level(level, sources):
        values = []
        for j, source in enumerate(sources):
            first = CHILD_START[level - 1] + 2 * j
            e = transfer[pl.ds(first, 2)].reshape(2 * RANK, RANK)
            values.append(jnp.dot(source, e, preferred_element_type=F32) * HALF_ROOT)
        return [
            jnp.concatenate(values[2 * q : 2 * q + 2], axis=1).astype(BF)
            for q in range(len(values) // 2)
        ]

    level1 = up_level(1, [h0[j] for j in range(PAIRS)])
    for q, block in enumerate(level1):
        level1_in[far, q] = block
    pl.semaphore_wait(barrier, N_LEAF - 1 + N_FAR - 1)
    ring_copy(0, 0).start()
    ring_copy(1, 0).start()
    sib_copy(2, 0).start()
    lax.fori_loop(0, LEAVES, start_x, 0)
    blocks = level1
    for level in range(2, 6):
        blocks = up_level(level, blocks)
        for q, block in enumerate(blocks):
            upper_in[far, ROW_START[level] // 2 - PIECE + q] = block
    e = transfer[pl.ds(CHILD_START[5], 2)].reshape(2 * RANK, RANK)
    root = (jnp.dot(blocks[0], e, preferred_element_type=F32) * HALF_ROOT).astype(BF)
    upper_in[far, PIECE - 1] = jnp.concatenate([root, jnp.zeros_like(root)], axis=1)
    roots[leaf] = folded(root)
    ring_copy(0, 1).start()
    ring_copy(1, 1).start()
    root_copies = []
    for k in range(1, N_LEAF):
        copy = pltpu.make_async_remote_copy(
            src_ref=roots.at[leaf],
            dst_ref=roots.at[leaf],
            send_sem=root_send.at[k],
            recv_sem=root_recv.at[k],
            device_id=(leaf_peer(k), far),
            device_id_type=MESH,
        )
        copy.start()
        root_copies.append(copy)
    sib_copy(2, 1).start()

    load_coupling.start()
    load_root_blocks.start()

    chunk = 1024

    def make_feats(q, carry):
        at = pl.ds(pl.multiple_of(q * chunk, chunk), chunk)
        c = coords[:, at].astype(F32)
        rows = [c[r : r + 1] for r in range(3)]
        square = rows[0] * rows[0] + rows[1] * rows[1] + rows[2] * rows[2]
        one = jnp.ones_like(square)
        feats = stacked_rows([*rows, one, one, one, *split3(square)], chunk)
        for t in range(chunk // P_SIZE):
            window[HALO + q * (chunk // P_SIZE) + t, RANK : RANK + FEATS] = feats[
                :, t * P_SIZE : (t + 1) * P_SIZE
            ]
        target_feats[:, at] = stacked_rows(
            [*(-2.0 * row for row in rows), *split3(square + SOFTEN), one, one, one], chunk
        )
        return carry

    lax.fori_loop(0, LEAVES * P_SIZE // chunk, make_feats, 0)

    lax.fori_loop(0, LEAVES, wait_x, 0)
    halo = []
    for way, src in enumerate((LEAVES, HALO)):
        copy = pltpu.make_async_remote_copy(
            src_ref=window.at[pl.ds(src, HALO)],
            dst_ref=halo_in.at[way],
            send_sem=halo_send.at[way],
            recv_sem=halo_recv.at[way],
            device_id=(leaf_peer(1 if way == 0 else -1), far),
            device_id_type=MESH,
        )
        copy.start()
        halo.append(copy)

    def spread(q, carry):
        block = jnp.concatenate(
            [window[8 * q + t, RANK : RANK + FEATS] for t in range(8)], axis=0
        )
        block = block.astype(F32).T
        for t in range(8):
            for c in range(3):
                at = t * FEATS + c
                source_coords[8 * q + t, c] = jnp.broadcast_to(
                    block[:, at : at + 1], (P_SIZE, P_SIZE)
                )
        return carry

    lax.fori_loop(HALO // 8, (HALO + LEAVES) // 8, spread, 0)

    def halo_arrived():
        for copy in halo:
            copy.wait()
        row = lax.broadcasted_iota(jnp.int32, (RANK + FEATS, P_SIZE), 0)
        blank = jnp.where((row >= RANK + 3) & (row < RANK + 6), 1.0, 0.0).astype(BF)
        for way, (edge, first) in enumerate(((0, 0), (N_LEAF - 1, HALO + LEAVES))):

            @pl.when(leaf == edge)
            def _():
                for t in range(HALO):
                    window[first + t] = blank

            @pl.when(leaf != edge)
            def _():
                for t in range(HALO):
                    window[first + t] = halo_in[way, t]

            lax.fori_loop(first // 8, (first + HALO) // 8, spread, 0)


    def top_up():
        for copy in root_copies:
            copy.wait()
        h = [unfolded(roots[g]) for g in range(N_LEAF)]
        for level in range(4):
            start = TOP_START[level]
            mapped = [
                jnp.dot(h[g], tops[start + g], preferred_element_type=F32)
                for g in range(len(h))
            ]
            h = [
                ((mapped[2 * g] + mapped[2 * g + 1]) * HALF_ROOT).astype(BF)
                for g in range(len(h) // 2)
            ]
        tops_in[far] = folded(h[0])

    def top_copy(k):
        block = tops_in.at[far]
        return pltpu.make_async_remote_copy(
            src_ref=block,
            dst_ref=block,
            send_sem=top_send.at[k],
            recv_sem=top_recv.at[k],
            device_id=(leaf, far_peer(k)),
            device_id_type=MESH,
        )

    def top_down():
        for k in range(1, N_FAR):
            top_copy(k).wait()
        load_root_blocks.wait()
        local = jnp.zeros((RANK, RANK), F32)
        for p in range(N_FAR):
            local = local + root_pattern[0, p].astype(F32) * jnp.dot(
                unfolded(tops_in[p]), root_blocks[p], preferred_element_type=F32
            )
        for level in reversed(range(4)):
            e = tops[TOP_START[level] + lax.shift_right_logical(leaf, level)]
            local = lax.dot_general(
                local.astype(BF), e, (((1,), (1,)), ((), ())), preferred_element_type=F32
            )
        descent[...] = local

    def near_leaf(i):
        target = target_feats[:, lanes(i)].astype(F32).T.astype(BF)
        c = coords[:, lanes(i)].astype(F32)
        own = [
            jnp.broadcast_to(c[r : r + 1], (P_SIZE, P_SIZE)).astype(BF) for r in range(3)
        ]
        total = jnp.zeros((RANK, P_SIZE), F32)
        for q in range(NEAR // 2):
            near = [offsets[2 * q + t, i] + (i + HALO) for t in range(2)]
            x = jnp.concatenate([window[at, 0:RANK] for at in near], axis=1)
            if q % 3 == 0:
                source = jnp.concatenate(
                    [window[at, RANK : RANK + FEATS] for at in near], axis=1
                )
                square = jnp.dot(target, source, preferred_element_type=F32)
                total = total + lax.dot_general(
                    x,
                    lax.rsqrt(square.astype(BF)),
                    (((1,), (1,)), ((), ())),
                    preferred_element_type=F32,
                )
            else:
                inverse = []
                for at in near:
                    d = [source_coords[at, r].astype(BF) - own[r] for r in range(3)]
                    square = d[0] * d[0] + jnp.asarray(SOFTEN, BF)
                    square = square + d[1] * d[1]
                    square = square + d[2] * d[2]
                    inverse.append(lax.rsqrt(square))
                total = total + jnp.dot(
                    x, jnp.concatenate(inverse, axis=0), preferred_element_type=F32
                )
        return total

    def near_group(step, carry):
        p = lax.rem(step + HALO // GROUP, GROUPS)
        for t in range(GROUP):
            near_sum[:, lanes(GROUP * p + t)] = near_leaf(GROUP * p + t)
        for group, events in AFTER_GROUP.items():

            @pl.when(step == group)
            def _():
                for event in events:
                    arrived(event)

        @pl.when(step == 2)
        def _():
            top_up()
            for k in range(1, N_FAR):
                top_copy(k).start()

        @pl.when(step == 6)
        def _():
            halo_arrived()

        @pl.when(step == 9)
        def _():
            top_down()

        return carry

    lax.fori_loop(0, GROUPS, near_group, 0)
    load_coupling.wait()

    def gain(row, parity, upper):
        half = slice(parity * RANK, (parity + 1) * RANK)
        ref, block = (upper_in, row // 2 - PIECE) if upper else (level1_in, row // 2)
        parts = [ref[pattern[k, row], block][:, half] for k in range(KC)]
        return jnp.dot(
            jnp.concatenate(parts, axis=1),
            coupling[row].reshape(KC * RANK, RANK),
            preferred_element_type=F32,
        )

    def others(upper):
        events = [(2, upper)]
        for event in range(EVENTS):
            if ROUTE[event][0] == upper:
                events += [(0, event), (1, event)]
        return events

    for way, event in others(1):
        sib_copy(way, event).wait_recv()

    def down(level, j, value):
        start = CHILD_START[level - 1]
        e = transfer[pl.ds(start + 2 * j, 2)].reshape(2 * RANK, RANK)
        both = lax.dot_general(
            value, e, (((1,), (1,)), ((), ())), preferred_element_type=F32
        )
        return both[:, :RANK], both[:, RANK:]

    values = [(descent[...] + gain(NODES - 1, 0, True)).astype(BF)]
    for level in range(6, 1, -1):
        children = []
        for j, value in enumerate(values):
            children += down(level, j, value)
        if level > 2:
            start = ROW_START[level - 1]
            values = [
                (child + gain(start + j, j % 2, True)).astype(BF)
                for j, child in enumerate(children)
            ]
    for j, child in enumerate(children):
        expansion[j] = child

    for event in (8, 9):
        arrived(event)
    for way, event in others(0):
        sib_copy(way, event).wait_recv()

    factor = 1.0 / math.sqrt(NEAR * P_SIZE)

    def finish(q, carry):
        for parity in range(2):
            j = 2 * q + parity
            value = (expansion[j] + gain(j, parity, False)).astype(BF)
            both = down(1, j, value)
            for t in range(2):
                at = lanes(2 * j + t)
                far_sum = jnp.dot(
                    both[t].astype(BF), basis[:, at], preferred_element_type=F32
                )
                out_vmem[:, at] = (near_sum[:, at] * factor + far_sum).astype(BF)
        return carry

    lax.fori_loop(0, PAIRS // 2, finish, 0, unroll=8)
    store = pltpu.make_async_copy(out_vmem, out_hbm, load_sem.at[0])
    store.start()
    for event in range(EVENTS):
        for way in range(2):
            ring_copy(way, event).wait_send()
    for way, event in others(0) + others(1):
        sib_copy(way, event).wait_send()
    store.wait()


def local(
    right_sides,
    point_coords,
    near_offsets,
    leaf_basis,
    local_transfer,
    top_transfer,
    coupling_pattern,
    coupling_blocks,
    root_pattern,
    root_blocks,
):
    smem = pl.BlockSpec(memory_space=pltpu.SMEM)
    vmem = pl.BlockSpec(memory_space=pltpu.VMEM)
    hbm = pl.BlockSpec(memory_space=pl.ANY)
    points = LEAVES * P_SIZE
    dma = pltpu.SemaphoreType.DMA
    out = pl.pallas_call(
        kernel,
        name="h2_product",
        out_shape=jax.ShapeDtypeStruct((RANK, points), BF),
        in_specs=[smem, smem, smem, vmem, vmem, hbm, hbm, hbm, hbm, hbm],
        out_specs=hbm,
        scratch_shapes=[
            pltpu.VMEM((WINDOW, RANK + FEATS, P_SIZE), BF),
            pltpu.VMEM((FEATS, points), BF),
            pltpu.VMEM((2, HALO, RANK + FEATS, P_SIZE), BF),
            pltpu.VMEM((WINDOW, 3, P_SIZE, P_SIZE), F32),
            pltpu.VMEM((RANK, points), BF),
            pltpu.VMEM((2 * NODES, RANK, RANK), BF),
            pltpu.VMEM((NODES, KC, RANK, RANK), BF),
            pltpu.VMEM((N_FAR, RANK, RANK), BF),
            pltpu.VMEM((PAIRS, RANK, 2 * RANK), BF),
            pltpu.VMEM((N_FAR, PIECE, RANK, 2 * RANK), BF),
            pltpu.VMEM((N_FAR, PIECE, RANK, 2 * RANK), BF),
            pltpu.VMEM((N_LEAF, RANK // 2, 2 * RANK), BF),
            pltpu.VMEM((N_FAR, RANK // 2, 2 * RANK), BF),
            pltpu.VMEM((RANK, RANK), F32),
            pltpu.VMEM((PAIRS, RANK, RANK), F32),
            pltpu.VMEM((RANK, points), F32),
            pltpu.VMEM((RANK, points), BF),
            dma((5,)),
            dma((LEAVES,)),
            dma((2,)),
            dma((2,)),
            dma((2, EVENTS)),
            dma((2, EVENTS)),
            dma((3, EVENTS)),
            dma((3, EVENTS)),
            dma((N_LEAF,)),
            dma((N_LEAF,)),
            dma((N_FAR,)),
            dma((N_FAR,)),
        ],
        compiler_params=pltpu.CompilerParams(
            collective_id=0, has_side_effects=True, vmem_limit_bytes=62 << 20
        ),
        cost_estimate=pl.CostEstimate(
            flops=4 << 30, bytes_accessed=16 << 20, transcendentals=25 << 20
        ),
    )(
        near_offsets[0].T,
        coupling_pattern[0].T,
        root_pattern,
        point_coords[0],
        top_transfer[0],
        right_sides[0],
        leaf_basis[0],
        local_transfer[0],
        coupling_blocks[0],
        root_blocks[0],
    )
    return out[None]


def solution(mesh):
    return jax.shard_map(
        local,
        mesh=mesh,
        in_specs=(
            P("far", None, "leaf"),
            P("far", None, "leaf"),
            P("far", "leaf", None),
            P("far", None, "leaf"),
            P("far", "leaf", None, None),
            P("far", None, None, None),
            P("far", "leaf", None),
            P("far", "leaf", None, None, None),
            P("far", None),
            P("far", None, None, None),
        ),
        out_specs=P("far", None, "leaf"),
        check_vma=False,
    )
```
